768 devices in a mesh: dp: 96 (over z, y_hi, x), fsdp: 8 (over y_lo, core).
Axes of the slice: x: 4, y: 8 (y_hi: 2, y_lo: 4; y = y_hi * 4 + y_lo), z: 12, core: 2. Of those that a mesh axis runs over, the one named last changes fastest.
Arguments:
- hidden_in: bfloat16 [24576, 8192], P('dp', 'fsdp'), may hold values from -6 to 6
- grad_out: bfloat16 [24576, 24576], P('dp', 'fsdp'), may hold values from -0.0234375 to 0.0234375
- basis: bfloat16 [8192, 512], P('fsdp'), may hold values from -0.25 to 0.25
- first_moment: float32 [24576, 512], P(('fsdp', 'dp')), may hold values from -1.5 to 1.5
- second_moment: float32 [24576, 512], P(('fsdp', 'dp')), may hold values from 0.0001 to 0.01
Outputs:
- new_first: float32 [24576, 512], P(('fsdp', 'dp'))
- new_second: float32 [24576, 512], P(('fsdp', 'dp'))
- update: bfloat16 [8, 3072, 8192], P(None, 'dp', 'fsdp')
The draws below stay inside these ranges and needn't reach their ends.
All inputs are finite; a program needn't handle non-finite values.
Results may differ from the reference program's by a relative error of at most 0.0058.
Values may be sent and summed in bfloat16 or wider, within the bound.
No kernel may reach another device: no remote copies, remote signals or barrier semaphores. Data moves between devices by JAX's collectives and lax.ppermute only.
A program may use at most 64 MiB of HBM per device.

```python
import math
import jax
import jax.numpy as jnp
from jax import lax

D = 8192
RANK = 512
STEP = 10
TOKENS = 24576
N_FSDP = 8


def steps_of(stream_key, dims, shards, smallest, largest):
    factor_of, own = 1.0, jax.random.fold_in(stream_key, 6)
    for position, parts in shards:
        steps = jnp.exp(jax.random.uniform(jax.random.fold_in(own, position), (parts,), jnp.float32, smallest / len(shards), largest / len(shards)))
        factor_of = factor_of * jnp.repeat(steps, dims[position] // parts).reshape([-1 if axis == position else 1 for axis in range(len(dims))])
    return factor_of


def normal_values(key, dims, width, limit, split=(), kind=jnp.bfloat16):
    array = jax.random.normal(key, dims, jnp.float32) * width
    if len(split) > 0:
        array = steps_of(key, dims, split, -0.22, 0.18) * array
    return jnp.clip(array, min=-limit, max=limit).astype(kind)


def setup_inputs(seed: int = 0) -> dict:
    keys = jax.random.split(jax.random.key(seed), 6)
    hidden_in = normal_values(keys[0], (TOKENS, D), 1.0, 6.0, ((0, 96), (1, 8)))
    grad_out = normal_values(keys[1], (TOKENS, 3 * D), (0.25 / TOKENS ** 0.5), 0.0234375, ((0, 96), (1, 8)))
    basis = normal_values(keys[2], (D, RANK), RANK ** -0.5, 0.25, ((0, 8),))
    first_moment = normal_values(keys[3], (3 * D, RANK), 0.1, 1.5, ((0, 768),), jnp.float32)
    second_moment = jnp.clip(jnp.exp(math.log(0.01) - 4.6051702 * jax.random.uniform(keys[4], (3 * D, RANK), jnp.float32) ** steps_of(keys[4], (3 * D, RANK), ((0, 768),), -0.2, 0.2)), 0.0001, 0.01)
    return dict(hidden_in=hidden_in, grad_out=grad_out, basis=basis, first_moment=first_moment, second_moment=second_moment)


def reference(hidden_in, grad_out, basis, first_moment, second_moment):
    reduced = jnp.dot(hidden_in, basis, preferred_element_type=jnp.float32).astype(jnp.bfloat16)
    projected = lax.dot_general(grad_out, reduced, (((0,), (0,)), ((), ())), preferred_element_type=jnp.float32)
    new_first = 0.9 * first_moment + 0.1 * projected
    new_second = 0.999 * second_moment + 0.001 * projected * projected
    first_hat = new_first / (1.0 - 0.9 ** STEP)
    second_hat = new_second / (1.0 - 0.999 ** STEP)
    direction = (first_hat / (jnp.sqrt(second_hat) + 1e-08)).astype(jnp.bfloat16)
    full = jnp.dot(direction, basis.T, preferred_element_type=jnp.float32).astype(jnp.bfloat16)
    update = full.reshape(N_FSDP, 3 * D // N_FSDP, D)
    return (new_first, new_second, update)
```

```python
import jax
import jax.numpy as jnp
from jax import lax
from jax.experimental import pallas as pl
from jax.experimental.pallas import tpu as pltpu
from jax.sharding import Mesh, PartitionSpec as P

STEP = 10
AXES = ("z", "h", "x", "y", "c")
SIZES = (12, 2, 4, 4, 2)
SWAP = ((0, 1), (1, 0))


def project(grad_ref, mine_ref, other_ref, out_ref):
    first = lax.axis_index("c") == 0
    total = None
    for x in range(grad_ref.shape[0]):
        mine, other = mine_ref[x], other_ref[x]
        low = jnp.where(first, mine, other)
        high = jnp.where(first, other, mine)
        reduced = jnp.concatenate([low, high], axis=0)
        term = jnp.dot(grad_ref[x], reduced, preferred_element_type=jnp.float32)
        total = term if total is None else total + term
    out_ref[...] = total.astype(out_ref.dtype)


def shards(hidden_in, grad_out, basis, first_moment, second_moment):
    f32, bf16 = jnp.float32, jnp.bfloat16
    rows = first_moment.shape[0]
    rank = basis.shape[1]
    tokens = hidden_in.shape[0]
    piece = tokens // 8
    turned = grad_out.T.reshape(24, 4, rows, tokens).transpose(1, 0, 2, 3).reshape(4, 24 * rows, tokens)

    partial = jnp.dot(hidden_in, basis, preferred_element_type=f32).astype(bf16)
    partial, turned = lax.optimization_barrier((partial, turned))
    spread = lax.all_to_all(turned, "x", 0, 0, tiled=True)
    partial = lax.all_to_all(partial, ("c", "y"), 0, 0, tiled=True).reshape(8, piece, rank)
    reduced = jnp.sum(partial.astype(f32), axis=0).astype(bf16)
    copies = jnp.broadcast_to(reduced[None], (16, piece, rank)).reshape(-1, rank)
    mine = lax.all_to_all(copies, ("x", "y"), 0, 0, tiled=True).reshape(4, 4 * piece, rank)
    other = lax.ppermute(mine, "c", SWAP)

    part = pl.pallas_call(
        project,
        out_shape=jax.ShapeDtypeStruct((24 * rows, rank), bf16),
        in_specs=[pl.BlockSpec(memory_space=pltpu.VMEM)] * 3,
        out_specs=pl.BlockSpec(memory_space=pltpu.VMEM),
        compiler_params=pltpu.CompilerParams(vmem_limit_bytes=32 * 1024 * 1024),
        cost_estimate=pl.CostEstimate(flops=2 * 24 * rows * 4 * tokens * rank, bytes_accessed=4 << 20, transcendentals=0),
    )(spread, mine, other)
    part = lax.all_to_all(part, ("z", "h"), 0, 0, tiled=True).reshape(24, rows, rank)
    projected = jnp.sum(part.astype(f32), axis=0)

    new_first = 0.9 * first_moment + 0.1 * projected
    new_second = 0.999 * second_moment + 0.001 * projected * projected
    first_hat = new_first / (1.0 - 0.9**STEP)
    second_hat = new_second / (1.0 - 0.999**STEP)
    direction = (first_hat / (jnp.sqrt(second_hat) + 1e-08)).astype(bf16)
    copies = jnp.broadcast_to(direction[None], (8, rows, rank)).reshape(-1, rank)
    grouped = lax.all_to_all(copies, ("y", "c"), 0, 0, tiled=True)
    update = lax.dot_general(grouped, basis, (((1,), (1,)), ((), ())), preferred_element_type=f32)
    return (new_first, new_second, update.astype(bf16).reshape(8, rows, -1))


def solution(mesh):
    fine = Mesh(mesh.devices.reshape(SIZES), AXES)
    dp, fsdp = ("z", "h", "x"), ("y", "c")
    in_specs = (P(dp, fsdp), P(dp, fsdp), P(fsdp, None), P(fsdp + dp, None), P(fsdp + dp, None))
    out_specs = (P(fsdp + dp, None), P(fsdp + dp, None), P(None, dp, fsdp))
    return jax.shard_map(shards, mesh=fine, in_specs=in_specs, out_specs=out_specs, check_vma=False)
```

```python
import jax
import jax.numpy as jnp
from jax import lax
from jax.experimental import pallas as pl
from jax.experimental.pallas import tpu as pltpu
from jax.sharding import Mesh, PartitionSpec as P

STEP = 10
AXES = ("z", "h", "x", "y", "c")
SIZES = (12, 2, 4, 4, 2)
SWAP = ((0, 1), (1, 0))
NEAR = ((0, 1), (1, 0), (2, 3), (3, 2))
FAR = ((0, 3), (3, 0), (1, 2), (2, 1))
RING = 4


def near(x):
    return x + 1 - 2 * lax.rem(x, 2)


def turn(grad_ref, keep_ref, near_ref, far_ref, turned):
    me = lax.axis_index("x")
    for block in range(grad_ref.shape[1] // 128):
        flipped = grad_ref[:, block * 128 : (block + 1) * 128].T
        for x in range(RING):
            turned[x, block * 32 : (block + 1) * 32, :] = flipped[x * 32 : (x + 1) * 32]
    width = keep_ref.shape[0]
    keep_ref[...] = turned[me]
    near_ref[:width] = turned[near(me)]
    far_ref[:width] = turned[RING - 1 - me]
    across = RING - 1 - near(me)
    near_ref[width:] = turned[across, : width // 2, :]
    far_ref[width:] = turned[across, width // 2 :, :]


def project(keep_ref, near_ref, far_ref, left_ref, right_ref, mine_ref, other_ref, out_ref):
    me = lax.axis_index("x")
    first = lax.axis_index("c") == 0
    width = keep_ref.shape[0]
    across = jnp.concatenate([left_ref[...], right_ref[...]], axis=0)
    sources = (
        (keep_ref[...], me),
        (near_ref[:width], near(me)),
        (far_ref[:width], RING - 1 - me),
        (across, RING - 1 - near(me)),
    )
    total = None
    for grad, x in sources:
        mine, other = mine_ref[x], other_ref[x]
        low = jnp.where(first, mine, other)
        high = jnp.where(first, other, mine)
        reduced = jnp.concatenate([low, high], axis=0)
        term = jnp.dot(grad, reduced, preferred_element_type=jnp.float32)
        total = term if total is None else total + term
    out_ref[...] = total.astype(out_ref.dtype)


def share(partial_ref, copies_ref):
    reduced = jnp.sum(partial_ref[...].astype(jnp.float32), axis=0).astype(copies_ref.dtype)
    for i in range(copies_ref.shape[0]):
        copies_ref[i] = reduced


def whole(kernel, ins, outs, scratch=(), flops=0):
    spec = pl.BlockSpec(memory_space=pltpu.VMEM)
    return pl.pallas_call(
        kernel,
        out_shape=outs,
        in_specs=[spec] * ins,
        out_specs=jax.tree.map(lambda _: spec, outs),
        scratch_shapes=scratch,
        compiler_params=pltpu.CompilerParams(vmem_limit_bytes=24 * 1024 * 1024),
        cost_estimate=pl.CostEstimate(flops=flops, bytes_accessed=4 << 20, transcendentals=0),
    )


def shards(hidden_in, grad_out, basis, first_moment, second_moment):
    f32, bf16 = jnp.float32, jnp.bfloat16
    rows = first_moment.shape[0]
    rank = basis.shape[1]
    tokens = hidden_in.shape[0]
    piece = tokens // 8
    width = 24 * rows
    shape = jax.ShapeDtypeStruct
    more = shape((width + width // 2, tokens), bf16)
    keep, to_near, to_far = whole(
        turn, 1, [shape((width, tokens), bf16), more, more], [pltpu.VMEM((RING, width, tokens), bf16)]
    )(grad_out)
    from_near = lax.ppermute(to_near, "x", NEAR)
    from_far = lax.ppermute(to_far, "x", FAR)

    partial = jnp.dot(hidden_in, basis, preferred_element_type=f32).astype(bf16)
    partial = lax.all_to_all(partial, ("c", "y"), 0, 0, tiled=True).reshape(8, piece, rank)
    partial, from_near, from_far = lax.optimization_barrier((partial, from_near, from_far))

    left = lax.ppermute(from_near[width:], "x", FAR)
    right = lax.ppermute(from_far[width:], "x", NEAR)
    copies = whole(share, 1, shape((16, piece, rank), bf16))(partial).reshape(-1, rank)
    mine = lax.all_to_all(copies, ("x", "y"), 0, 0, tiled=True).reshape(4, 4 * piece, rank)
    mine, left, right = lax.optimization_barrier((mine, left, right))
    other = lax.ppermute(mine, "c", SWAP)

    part = whole(project, 7, shape((width, rank), bf16), flops=2 * width * 4 * tokens * rank)(
        keep, from_near, from_far, left, right, mine, other
    )
    part = lax.all_to_all(part, ("z", "h"), 0, 0, tiled=True).reshape(24, rows, rank)
    projected = jnp.sum(part.astype(f32), axis=0)

    new_first = 0.9 * first_moment + 0.1 * projected
    new_second = 0.999 * second_moment + 0.001 * projected * projected
    first_hat = new_first / (1.0 - 0.9**STEP)
    second_hat = new_second / (1.0 - 0.999**STEP)
    direction = (first_hat / (jnp.sqrt(second_hat) + 1e-08)).astype(bf16)
    copies = jnp.broadcast_to(direction[None], (8, rows, rank)).reshape(-1, rank)
    grouped = lax.all_to_all(copies, ("y", "c"), 0, 0, tiled=True)
    update = lax.dot_general(grouped, basis, (((1,), (1,)), ((), ())), preferred_element_type=f32)
    return (new_first, new_second, update.astype(bf16).reshape(8, rows, -1))


def solution(mesh):
    fine = Mesh(mesh.devices.reshape(SIZES), AXES)
    dp, fsdp = ("z", "h", "x"), ("y", "c")
    in_specs = (P(dp, fsdp), P(dp, fsdp), P(fsdp, None), P(fsdp + dp, None), P(fsdp + dp, None))
    out_specs = (P(fsdp + dp, None), P(fsdp + dp, None), P(None, dp, fsdp))
    return jax.shard_map(shards, mesh=fine, in_specs=in_specs, out_specs=out_specs, check_vma=False)
```

```python
import jax
import jax.numpy as jnp
from jax import lax
from jax.experimental import pallas as pl
from jax.experimental.pallas import tpu as pltpu
from jax.sharding import Mesh, PartitionSpec as P

STEP = 10
AXES = ("z", "h", "x", "y", "c")
SIZES = (12, 2, 4, 4, 2)
SWAP = ((0, 1), (1, 0))
NEAR = ((0, 1), (1, 0), (2, 3), (3, 2))
FAR = ((0, 3), (3, 0), (1, 2), (2, 1))
RING = 4


def near(x):
    return x + 1 - 2 * lax.rem(x, 2)


def turn(grad_ref, keep_ref, near_ref, far_ref, turned):
    me = lax.axis_index("x")
    for block in range(grad_ref.shape[1] // 128):
        flipped = grad_ref[:, block * 128 : (block + 1) * 128].T
        for x in range(RING):
            turned[x, block * 32 : (block + 1) * 32, :] = flipped[x * 32 : (x + 1) * 32]
    width = keep_ref.shape[0]
    keep_ref[...] = turned[me]
    near_ref[:width] = turned[near(me)]
    far_ref[:width] = turned[RING - 1 - me]
    across = RING - 1 - near(me)
    near_ref[width:] = turned[across, : width // 2, :]
    far_ref[width:] = turned[across, width // 2 :, :]


def project(keep_ref, near_ref, far_ref, left_ref, right_ref, mine_ref, other_ref, out_ref):
    me = lax.axis_index("x")
    first = lax.axis_index("c") == 0
    width = keep_ref.shape[0]
    across = jnp.concatenate([left_ref[...], right_ref[...]], axis=0)
    sources = (
        (keep_ref[...], me),
        (near_ref[:width], near(me)),
        (far_ref[:width], RING - 1 - me),
        (across, RING - 1 - near(me)),
    )
    total = None
    for grad, x in sources:
        mine, other = mine_ref[x], other_ref[x]
        low = jnp.where(first, mine, other)
        high = jnp.where(first, other, mine)
        reduced = jnp.concatenate([low, high], axis=0)
        term = jnp.dot(grad, reduced, preferred_element_type=jnp.float32)
        total = term if total is None else total + term
    out_ref[...] = total.astype(out_ref.dtype)


def share(partial_ref, copies_ref):
    reduced = jnp.sum(partial_ref[...].astype(jnp.float32), axis=0).astype(copies_ref.dtype)
    for i in range(copies_ref.shape[0]):
        copies_ref[i] = reduced


def whole(kernel, ins, outs, scratch=(), flops=0):
    spec = pl.BlockSpec(memory_space=pltpu.VMEM)
    return pl.pallas_call(
        kernel,
        out_shape=outs,
        in_specs=[spec] * ins,
        out_specs=jax.tree.map(lambda _: spec, outs),
        scratch_shapes=scratch,
        compiler_params=pltpu.CompilerParams(vmem_limit_bytes=24 * 1024 * 1024),
        cost_estimate=pl.CostEstimate(flops=flops, bytes_accessed=4 << 20, transcendentals=0),
    )


def shards(hidden_in, grad_out, basis, first_moment, second_moment):
    f32, bf16 = jnp.float32, jnp.bfloat16
    rows = first_moment.shape[0]
    rank = basis.shape[1]
    tokens = hidden_in.shape[0]
    piece = tokens // 8
    width = 24 * rows
    shape = jax.ShapeDtypeStruct
    more = shape((width + width // 2, tokens), bf16)
    keep, to_near, to_far = whole(
        turn, 1, [shape((width, tokens), bf16), more, more], [pltpu.VMEM((RING, width, tokens), bf16)]
    )(grad_out)
    from_near = lax.ppermute(to_near, "x", NEAR)
    from_far = lax.ppermute(to_far, "x", FAR)

    partial = jnp.dot(hidden_in, basis, preferred_element_type=f32).astype(bf16)
    partial = lax.all_to_all(partial, ("c", "y"), 0, 0, tiled=True).reshape(8, piece, rank)
    partial, from_near, from_far = lax.optimization_barrier((partial, from_near, from_far))

    left = lax.ppermute(from_near[width:], "x", FAR)
    right = lax.ppermute(from_far[width:], "x", NEAR)
    copies = whole(share, 1, shape((16, piece, rank), bf16))(partial).reshape(-1, rank)
    mine = lax.all_to_all(copies, ("x", "y"), 0, 0, tiled=True).reshape(4, 4 * piece, rank)
    mine, left, right = lax.optimization_barrier((mine, left, right))
    other = lax.ppermute(mine, "c", SWAP)

    part = whole(project, 7, shape((width, rank), bf16), flops=2 * width * 4 * tokens * rank)(
        keep, from_near, from_far, left, right, mine, other
    )
    part = lax.all_to_all(part, ("z", "h"), 0, 0, tiled=True).reshape(24, rows, rank)
    projected = jnp.sum(part.astype(f32), axis=0)

    new_first = 0.9 * first_moment + 0.1 * projected
    new_second = 0.999 * second_moment + 0.001 * projected * projected
    first_hat = new_first / (1.0 - 0.9**STEP)
    second_hat = new_second / (1.0 - 0.999**STEP)
    direction = (first_hat / (jnp.sqrt(second_hat) + 1e-08)).astype(bf16)
    copies = jnp.broadcast_to(direction[None], (4, rows, rank)).reshape(-1, rank)
    grouped = lax.all_to_all(copies, "y", 0, 0, tiled=True).reshape(4, rows, rank)
    grouped = lax.all_gather(grouped, "c", axis=1, tiled=False).reshape(8 * rows, rank)
    update = lax.dot_general(grouped, basis, (((1,), (1,)), ((), ())), preferred_element_type=f32)
    return (new_first, new_second, update.astype(bf16).reshape(8, rows, -1))


def solution(mesh):
    fine = Mesh(mesh.devices.reshape(SIZES), AXES)
    dp, fsdp = ("z", "h", "x"), ("y", "c")
    in_specs = (P(dp, fsdp), P(dp, fsdp), P(fsdp, None), P(fsdp + dp, None), P(fsdp + dp, None))
    out_specs = (P(fsdp + dp, None), P(fsdp + dp, None), P(None, dp, fsdp))
    return jax.shard_map(shards, mesh=fine, in_specs=in_specs, out_specs=out_specs, check_vma=False)
```

```python
import jax
import jax.numpy as jnp
from jax import lax
from jax.experimental import pallas as pl
from jax.experimental.pallas import tpu as pltpu
from jax.sharding import Mesh, PartitionSpec as P

STEP = 10
AXES = ("zh", "zl", "h", "x", "y", "c")
SIZES = (4, 3, 2, 4, 4, 2)
GROUP = 3
SWAP = ((0, 1), (1, 0))
NEAR = ((0, 1), (1, 0), (2, 3), (3, 2))
FAR = ((0, 3), (3, 0), (1, 2), (2, 1))
RING = 4


def near(x):
    return x + 1 - 2 * lax.rem(x, 2)


def turn(grad_ref, keep_ref, near_ref, far_ref, turned):
    me, mine = lax.axis_index("x"), lax.axis_index("zl")
    part = turned.shape[1] // GROUP
    for block in range(grad_ref.shape[1] // 128):
        flipped = grad_ref[:, block * 128 : (block + 1) * 128].T
        slot = lax.rem(block // 2 % GROUP + GROUP - mine, GROUP)
        row = slot * part + (block // (2 * GROUP) * 2 + block % 2) * 32
        at = pl.ds(pl.multiple_of(row, 32), 32)
        for x in range(RING):
            turned[x, at, :] = flipped[x * 32 : (x + 1) * 32]
    width = keep_ref.shape[0]
    keep_ref[...] = turned[me]
    near_ref[:width] = turned[near(me)]
    far_ref[:width] = turned[RING - 1 - me]
    across = RING - 1 - near(me)
    near_ref[width:] = turned[across, : width // 2, :]
    far_ref[width:] = turned[across, width // 2 :, :]


def project(keep_ref, near_ref, far_ref, left_ref, right_ref, mine_ref, other_ref, own_ref, *sends):
    me = lax.axis_index("x")
    first = lax.axis_index("c") == 0
    width = keep_ref.shape[0]
    across = jnp.concatenate([left_ref[...], right_ref[...]], axis=0)
    sources = (
        (keep_ref[...], me),
        (near_ref[:width], near(me)),
        (far_ref[:width], RING - 1 - me),
        (across, RING - 1 - near(me)),
    )
    total = None
    for grad, x in sources:
        mine, other = mine_ref[x], other_ref[x]
        low = jnp.where(first, mine, other)
        high = jnp.where(first, other, mine)
        reduced = jnp.concatenate([low, high], axis=0)
        term = jnp.dot(grad, reduced, preferred_element_type=jnp.float32)
        total = term if total is None else total + term
    part = own_ref.shape[0]
    own_ref[...] = total[:part]
    for k, send_ref in enumerate(sends, 1):
        send_ref[...] = total[k * part : (k + 1) * part].astype(send_ref.dtype)


def share(partial_ref, copies_ref):
    reduced = jnp.sum(partial_ref[...].astype(jnp.float32), axis=0).astype(copies_ref.dtype)
    for i in range(copies_ref.shape[0]):
        copies_ref[i] = reduced


def whole(kernel, ins, outs, scratch=(), flops=0):
    spec = pl.BlockSpec(memory_space=pltpu.VMEM)
    return pl.pallas_call(
        kernel,
        out_shape=outs,
        in_specs=[spec] * ins,
        out_specs=jax.tree.map(lambda _: spec, outs),
        scratch_shapes=scratch,
        compiler_params=pltpu.CompilerParams(vmem_limit_bytes=24 * 1024 * 1024),
        cost_estimate=pl.CostEstimate(flops=flops, bytes_accessed=4 << 20, transcendentals=0),
    )


def shards(hidden_in, grad_out, basis, first_moment, second_moment):
    f32, bf16 = jnp.float32, jnp.bfloat16
    rows = first_moment.shape[0]
    rank = basis.shape[1]
    tokens = hidden_in.shape[0]
    piece = tokens // 8
    width = 24 * rows
    shape = jax.ShapeDtypeStruct
    more = shape((width + width // 2, tokens), bf16)
    keep, to_near, to_far = whole(
        turn, 1, [shape((width, tokens), bf16), more, more], [pltpu.VMEM((RING, width, tokens), bf16)]
    )(grad_out)
    from_near = lax.ppermute(to_near, "x", NEAR)
    from_far = lax.ppermute(to_far, "x", FAR)

    partial = jnp.dot(hidden_in, basis, preferred_element_type=f32).astype(bf16)
    partial = lax.all_to_all(partial, ("c", "y"), 0, 0, tiled=True).reshape(8, piece, rank)
    partial, from_near, from_far = lax.optimization_barrier((partial, from_near, from_far))

    left = lax.ppermute(from_near[width:], "x", FAR)
    right = lax.ppermute(from_far[width:], "x", NEAR)
    copies = whole(share, 1, shape((16, piece, rank), bf16))(partial).reshape(-1, rank)
    mine = lax.all_to_all(copies, ("x", "y"), 0, 0, tiled=True).reshape(4, 4 * piece, rank)
    mine, left, right = lax.optimization_barrier((mine, left, right))
    other = lax.ppermute(mine, "c", SWAP)

    part = width // GROUP
    own, *sends = whole(
        project,
        7,
        [shape((part, rank), f32)] + [shape((part, rank), bf16)] * (GROUP - 1),
        flops=2 * width * 4 * tokens * rank,
    )(keep, from_near, from_far, left, right, mine, other)
    for k, send in enumerate(sends, 1):
        own = own + lax.ppermute(send, "zl", [(z, (z + k) % GROUP) for z in range(GROUP)]).astype(f32)
    part = lax.all_to_all(own.astype(bf16), ("zh", "h"), 0, 0, tiled=True).reshape(24 // GROUP, rows, rank)
    projected = jnp.sum(part.astype(f32), axis=0)

    new_first = 0.9 * first_moment + 0.1 * projected
    new_second = 0.999 * second_moment + 0.001 * projected * projected
    first_hat = new_first / (1.0 - 0.9**STEP)
    second_hat = new_second / (1.0 - 0.999**STEP)
    direction = (first_hat / (jnp.sqrt(second_hat) + 1e-08)).astype(bf16)
    copies = jnp.broadcast_to(direction[None], (4, rows, rank)).reshape(-1, rank)
    grouped = lax.all_to_all(copies, "y", 0, 0, tiled=True).reshape(4, rows, rank)
    grouped = lax.all_gather(grouped, "c", axis=1, tiled=False).reshape(8 * rows, rank)
    update = lax.dot_general(grouped, basis, (((1,), (1,)), ((), ())), preferred_element_type=f32)
    return (new_first, new_second, update.astype(bf16).reshape(8, rows, -1))


def solution(mesh):
    fine = Mesh(mesh.devices.reshape(SIZES), AXES)
    dp, fsdp = ("zh", "zl", "h", "x"), ("y", "c")
    in_specs = (P(dp, fsdp), P(dp, fsdp), P(fsdp, None), P(fsdp + dp, None), P(fsdp + dp, None))
    out_specs = (P(fsdp + dp, None), P(fsdp + dp, None), P(None, dp, fsdp))
    return jax.shard_map(shards, mesh=fine, in_specs=in_specs, out_specs=out_specs, check_vma=False)
```
